32 devices in a mesh: dp: 4 (over y, core), seq: 8 (over z, x).
Axes of the slice: x: 2, y: 2, z: 4, core: 2. Of those that a mesh axis runs over, the one named last changes fastest.
Arguments:
- inputs: bfloat16 [4, 1536, 768], P('dp', 'seq'), may hold values from -6 to 6
- cotangent: bfloat16 [4, 1536, 768], P('dp', 'seq'), may hold values from -6 to 6
- dilated_kernel_weight: bfloat16 [768, 3, 384], P('dp'), may hold values from -0.125 to 0.125
- point_weight: bfloat16 [384, 768], P('dp'), may hold values from -0.3125 to 0.3125
Outputs:
- grad_input: bfloat16 [4, 1536, 768], P('dp', 'seq')
- kernel_weight_gradient: float32 [768, 3, 384], P('dp')
- pointwise_weight_gradient: float32 [384, 768], P('dp')
The draws below stay inside these ranges and needn't reach their ends.
All inputs are finite; a program needn't handle non-finite values.
Results may differ from the reference program's by a relative error of at most 0.0054.
Values may be sent and summed in bfloat16 or wider, within the bound.
A program may use at most 64 MiB of HBM per device.

```python
import jax
import jax.numpy as jnp
from jax import lax

C = 768
CI = 384
DILATION_SPAN = 32
SEQS = 4
BINS = 1536


def strengthened(entries, key, source, target, parts, factor):
    def block_of(dim):
        return (jnp.arange(entries.shape[dim]) // (entries.shape[dim] // parts)).reshape((-1,) + (1,) * (entries.ndim - 1 - dim))

    near = jax.random.permutation(key, parts)[block_of(target)]
    other_side = (block_of(target) + parts // 2) % parts
    return jnp.where((block_of(source) == near) | (block_of(source) == other_side), factor * entries, entries)


def levels(key, dims, cuts, least, high):
    factor_of, own = 1.0, jax.random.fold_in(key, 6)
    for position, blocks in cuts:
        draws = jnp.exp(jax.random.uniform(jax.random.fold_in(own, position), (blocks,), jnp.float32, least / len(cuts), high / len(cuts)))
        factor_of = factor_of * jnp.repeat(draws, dims[position] // blocks).reshape([-1 if axis == position else 1 for axis in range(len(dims))])
    return factor_of


def centred(stream_key, extent, width, limit, pieces=(), kind=jnp.bfloat16):
    entries = width * jax.random.normal(stream_key, extent, jnp.float32)
    if pieces:
        entries = entries * levels(stream_key, extent, pieces, -0.22, 0.18)
    return jnp.clip(entries, -limit, limit).astype(kind)


def gaussian_with(stream_key, dims, deviation, most, cuts, heavy, dtype=jnp.bfloat16):
    result = deviation * jax.random.normal(stream_key, dims, jnp.float32)
    if cuts:
        result = result * levels(stream_key, dims, cuts, -0.22, 0.18)
    return jnp.clip(strengthened(result, jax.random.fold_in(stream_key, 3), *heavy), -most, most).astype(dtype)


def setup_inputs(seed: int = 0) -> dict:
    seeds = jax.random.split(jax.random.key(seed), 5)
    inputs = centred(seeds[0], (SEQS, BINS, C), 1.0, 6.0, ((0, 4), (1, 8)))
    cotangent = gaussian_with(seeds[1], (SEQS, BINS, C), 1.0, 6.0, ((0, 4), (1, 8)), (1, 2, 8, 2.0))
    dilated_kernel_weight = centred(seeds[2], (C, 3, CI), (3 * C) ** -0.5, 0.125, ((0, 4),))
    point_weight = centred(seeds[3], (CI, C), CI ** -0.5, 0.3125, ((0, 4),))
    return dict(inputs=inputs, cotangent=cotangent, dilated_kernel_weight=dilated_kernel_weight, point_weight=point_weight)


def gelu_apply(values):
    return jax.nn.gelu(values, approximate=True)

def rms_normed(values):
    return values * lax.rsqrt(lax.optimization_barrier(jnp.mean(values * values, axis=-1, keepdims=True)) + 1e-06)

def reference(inputs, cotangent, dilated_kernel_weight, point_weight):

    def per_sequence(totals, sample_pair):
        seq_inputs, seq_cot = sample_pair
        input_length = seq_inputs.shape[0]
        normal, pull_norm = jax.vjp(rms_normed, seq_inputs.astype(jnp.float32))
        activated_hidden, pull_act = jax.vjp(gelu_apply, normal)
        padded_activation = jnp.pad(activated_hidden.astype(jnp.bfloat16), ((DILATION_SPAN, DILATION_SPAN), (0, 0)))
        preactivation = sum((jnp.dot(padded_activation[kernel_tap_index * DILATION_SPAN:kernel_tap_index * DILATION_SPAN + input_length], dilated_kernel_weight[:, kernel_tap_index, :], preferred_element_type=jnp.float32) for kernel_tap_index in range(3)))
        hidden, pull_hidden = jax.vjp(gelu_apply, preactivation)
        hidden_halfprec = hidden.astype(jnp.bfloat16)
        pointwise_weight_gradient = jnp.dot(hidden_halfprec.T, seq_cot, preferred_element_type=jnp.float32)
        upstream_gradient = jnp.dot(seq_cot, point_weight.T, preferred_element_type=jnp.float32)
        delta_rows = pull_hidden(upstream_gradient)[0].astype(jnp.bfloat16)
        kernel_weight_gradient = jnp.stack([jnp.dot(padded_activation[kernel_tap_index * DILATION_SPAN:kernel_tap_index * DILATION_SPAN + input_length].T, delta_rows, preferred_element_type=jnp.float32) for kernel_tap_index in range(3)], axis=1)
        padded_delta = jnp.pad(delta_rows, ((DILATION_SPAN, DILATION_SPAN), (0, 0)))
        activation_gradient = sum((jnp.dot(padded_delta[(2 - kernel_tap_index) * DILATION_SPAN:(2 - kernel_tap_index) * DILATION_SPAN + input_length], dilated_kernel_weight[:, kernel_tap_index, :].T, preferred_element_type=jnp.float32) for kernel_tap_index in range(3)))
        grad_normal = pull_act(activation_gradient)[0]
        grad_inner = pull_norm(grad_normal)[0]
        grad_input = (seq_cot.astype(jnp.float32) + grad_inner).astype(jnp.bfloat16)
        return ((totals[0] + kernel_weight_gradient, totals[1] + pointwise_weight_gradient), grad_input)
    start = (jnp.zeros(dilated_kernel_weight.shape, jnp.float32), jnp.zeros(point_weight.shape, jnp.float32))
    (kernel_weight_gradient, pointwise_weight_gradient), grad_input = lax.scan(per_sequence, start, (inputs, cotangent))
    return (grad_input, kernel_weight_gradient, pointwise_weight_gradient)
```

```python
import functools

import jax
import jax.numpy as jnp
from jax import lax
from jax.experimental import pallas as pl
from jax.experimental.pallas import tpu as pltpu
from jax.sharding import PartitionSpec as P

DILATION_SPAN = 32
MESH = pl.DeviceIdType.MESH
F32, BF16 = jnp.float32, jnp.bfloat16
GELU_SCALE, GELU_CUBIC = (2.0 / jnp.pi) ** 0.5, 0.044715


def extended(x, sides, width):
    for axis, dim in sides:
        size, length = (lax.axis_size(axis), x.shape[dim])
        up = [(i, (i + 1) % size) for i in range(size - 1)]
        down = [(j, i) for i, j in up]
        last = lax.slice_in_dim(x, length - width, length, axis=dim)
        initial = lax.slice_in_dim(x, 0, width, axis=dim)
        before = lax.ppermute(last, axis, up)
        after = lax.ppermute(initial, axis, down)
        x = jnp.concatenate([before, x, after], axis=dim)
    return x


def gelu_apply(values):
    return jax.nn.gelu(values, approximate=True)


def rms_normed(values):
    return values * lax.rsqrt(jnp.mean(values * values, axis=-1, keepdims=True) + 1e-06)


def conv_forward(padded_activation, weight_full, output_length):
    return sum(
        (
            jnp.einsum(
                "amv,vb->amb",
                padded_activation[
                    :,
                    kernel_tap_index * DILATION_SPAN : kernel_tap_index * DILATION_SPAN
                    + output_length,
                ],
                weight_full[:, kernel_tap_index, :],
                preferred_element_type=jnp.float32,
            )
            for kernel_tap_index in range(3)
        )
    )


def conv_weight_grad(padded_activation, delta_rows, input_length):
    return jnp.stack(
        [
            jnp.einsum(
                "hyr,hyk->rk",
                padded_activation[
                    :,
                    kernel_tap_index * DILATION_SPAN : kernel_tap_index * DILATION_SPAN
                    + input_length,
                ],
                delta_rows,
                preferred_element_type=jnp.float32,
            )
            for kernel_tap_index in range(3)
        ],
        axis=1,
    )


def conv_backward(padded_delta, weight_full, input_length):
    return sum(
        (
            jnp.einsum(
                "mfi,xi->mfx",
                padded_delta[
                    :,
                    (2 - kernel_tap_index) * DILATION_SPAN : (2 - kernel_tap_index) * DILATION_SPAN
                    + input_length,
                ],
                weight_full[:, kernel_tap_index, :],
                preferred_element_type=jnp.float32,
            )
            for kernel_tap_index in range(3)
        )
    )


def per_device(inputs, cotangent, dilated_kernel_weight, point_weight):
    conv_full, pointwise_full_weight = (
        lax.all_gather(dilated_kernel_weight, "dp", axis=0, tiled=True),
        lax.all_gather(point_weight, "dp", axis=0, tiled=True),
    )
    input_length = inputs.shape[1]
    normal, pull_norm = jax.vjp(rms_normed, inputs.astype(jnp.float32))
    activated_hidden, pull_act = jax.vjp(gelu_apply, normal)
    padded_activation = extended(
        activated_hidden.astype(jnp.bfloat16), (("seq", 1),), DILATION_SPAN
    )
    preactivation = conv_forward(padded_activation, conv_full, input_length)
    hidden, pull_hidden = jax.vjp(gelu_apply, preactivation)
    hidden_halfprec = hidden.astype(jnp.bfloat16)
    pointwise_weight_gradient = jnp.einsum(
        "xth,xtr->hr", hidden_halfprec, cotangent, preferred_element_type=jnp.float32
    )
    upstream_gradient = jnp.einsum(
        "pqy,oy->pqo", cotangent, pointwise_full_weight, preferred_element_type=jnp.float32
    )
    delta_rows = pull_hidden(upstream_gradient)[0].astype(jnp.bfloat16)
    kernel_weight_gradient = conv_weight_grad(padded_activation, delta_rows, input_length)
    padded_delta = extended(delta_rows, (("seq", 1),), DILATION_SPAN)
    activation_gradient = conv_backward(padded_delta, conv_full, input_length)
    grad_normal = pull_act(activation_gradient)[0]
    grad_inner = pull_norm(grad_normal)[0]
    grad_input = (cotangent.astype(jnp.float32) + grad_inner).astype(jnp.bfloat16)
    owned_conv, owned_point = (
        lax.psum_scatter(kernel_weight_gradient, "dp", scatter_dimension=0, tiled=True),
        lax.psum_scatter(pointwise_weight_gradient, "dp", scatter_dimension=0, tiled=True),
    )
    owned_conv, owned_point = lax.psum((owned_conv, owned_point), "seq")
    return (grad_input, owned_conv, owned_point)


def gelu_and_slope(v):
    square = v * v
    t = jnp.tanh(GELU_SCALE * v * (1.0 + GELU_CUBIC * square))
    half = 0.5 * (1.0 + t)
    slope = half + 0.5 * GELU_SCALE * v * (1.0 - t * t) * (1.0 + 3.0 * GELU_CUBIC * square)
    return v * half, slope


def normed(values):
    scale = lax.rsqrt(jnp.mean(values * values, axis=-1, keepdims=True) + 1e-06)
    return values * scale, scale


def dot(a, b, contract):
    return lax.dot_general(a, b, (contract, ((), ())), preferred_element_type=F32)


NN, NT, TN = ((1,), (0,)), ((1,), (1,)), ((0,), (0,))


def fused_kernel(
    seq,
    x_ref,
    cot_ref,
    wk_ref,
    wp_ref,
    gin_ref,
    grads_ref,
    weights,
    x_halo,
    act,
    delta,
    partial,
    core_out,
    core_in,
    y_out,
    y_in,
    y_own,
    x_out,
    x_in,
    z_own,
    z_out,
    z_in,
    total,
    send_sem,
    recv_sem,
):
    span = DILATION_SPAN
    bins, channels = x_ref.shape
    pieces, _, ci = weights.shape
    rows = wk_ref.shape[1]
    half = rows // 2
    nz = seq // 2
    chunk = rows // nz
    d, s = lax.axis_index("dp"), lax.axis_index("seq")
    y, c = d // 2, d % 2
    z, x = s // 2, s % 2
    sibling = (2 * y + 1 - c, s)
    across_y = (2 * (1 - y) + c, s)
    across_x = (d, 2 * z + 1 - x)
    after, before = (d, (s + 1) % seq), (d, (s + seq - 1) % seq)
    z_peer = [(z + r) % nz for r in range(1, nz)]

    count = [0]
    sent = []

    def copy(src, dst, device):
        i = count[0]
        count[0] += 1
        op = pltpu.make_async_remote_copy(
            src_ref=src,
            dst_ref=dst,
            send_sem=send_sem.at[i],
            recv_sem=recv_sem.at[i],
            device_id=device,
            device_id_type=MESH,
        )
        op.start()
        sent.append(op)
        return op

    def at(start, size, step=16):
        return pl.ds(pl.multiple_of(start, step), size)

    own = rows * d
    weights[0, at(own, half), :] = wp_ref[:, :ci]
    weights[0, at(own + half, half), :] = wp_ref[:, ci:]
    for k in range(3):
        weights[1 + k, at(own, rows), :] = wk_ref[k]

    barrier = pltpu.get_barrier_semaphore()
    peers = [sibling, across_y, across_x, after, before] + [(d, 2 * j + x) for j in z_peer]
    for device in peers:
        pl.semaphore_signal(barrier, inc=1, device_id=device, device_id_type=MESH)
    pl.semaphore_wait(barrier, len(peers))

    def block(g, start, size):
        return weights.at[2 * g : 2 * g + 2, at(start, size), :]

    def same(ref, device):
        return copy(ref, ref, device)

    groups = range(pieces // 2)
    w_y = [same(block(g, own + half * x, half), across_y) for g in groups]
    halo_after = copy(x_ref.at[bins - span :, :], x_halo.at[0], after)
    halo_before = copy(x_ref.at[:span, :], x_halo.at[1], before)
    w_core = [same(block(g, own, rows), sibling) for g in groups]

    normal, _ = normed(x_ref[...].astype(F32))
    act[span : span + bins, :] = gelu_and_slope(normal)[0].astype(BF16)

    other = rows * (2 * (1 - y) + c)
    w_x, w_pass = [], []
    for g in groups:
        w_y[g].wait_recv()
        w_x.append(same(block(g, other + half * x, half), across_x))
        w_pass.append(same(block(g, other + half * x, half), sibling))
    halo_after.wait_recv()
    halo_before.wait_recv()
    for i, edge, start in ((0, 0, 0), (1, seq - 1, span + bins)):
        side, _ = normed(x_halo[i].astype(F32))
        side = gelu_and_slope(side)[0]
        act[start : start + span, :] = jnp.where(s == edge, 0.0, side).astype(BF16)
    w_last = []
    for g in groups:
        w_x[g].wait_recv()
        w_last.append(same(block(g, other + half * (1 - x), half), sibling))
    for g in groups:
        w_core[g].wait_recv()
        w_pass[g].wait_recv()
        w_last[g].wait_recv()

    cot = cot_ref[...]
    preact = sum(dot(act[span * k : span * k + bins, :], weights[1 + k], NN) for k in range(3))
    hidden, slope = gelu_and_slope(preact)
    hidden = hidden.astype(BF16)

    def core_step(p):
        for i in range(2):
            core_out[p, rows * i : rows * (i + 1), :] = partial[
                p, at(rows * (2 * i + 1 - c), rows), :
            ].astype(BF16)
        return copy(core_out.at[p], core_in.at[p], sibling)

    def y_step(p):
        core[p].wait_recv()
        y_out[p] = (
            partial[p, at(rows * (2 * (1 - y) + c), rows), :]
            + core_in[p, at(rows * (1 - y), rows), :].astype(F32)
        ).astype(BF16)
        op = copy(y_out.at[p], y_in.at[p], across_y)
        y_own[p] = partial[p, at(own, rows), :] + core_in[p, at(rows * y, rows), :].astype(F32)
        return op

    def x_step(p):
        over_y[p].wait_recv()
        theirs, mine = at(half * (1 - x), half), at(half * x, half)
        x_out[p] = (y_own[p, theirs, :] + y_in[p, theirs, :].astype(F32)).astype(BF16)
        op = copy(x_out.at[p], x_in.at[p], across_x)
        z_own[p] = y_own[p, mine, :] + y_in[p, mine, :].astype(F32)
        return op

    def z_step(g):
        for p in (2 * g, 2 * g + 1):
            over_x[p].wait_recv()
            z_own[p] = z_own[p] + x_in[p].astype(F32)
            z_out[p] = z_own[p].astype(BF16)
        ops = []
        for r, j in enumerate(z_peer):
            piece, row = j // (nz // 2), chunk * (j % (nz // 2))
            ops.append(copy(z_out.at[2 * g + piece, at(row, chunk), :], z_in.at[g, r], (d, 2 * j + x)))
        return ops

    def spread_z(g):
        piece, row = 2 * g + z // (nz // 2), chunk * (z % (nz // 2))
        summed = z_own[piece, at(row, chunk), :]
        for r in range(nz - 1):
            over_z[g][r].wait_recv()
            summed = summed + z_in[g, r].astype(F32)
        place = total.at[piece, at(half * x + row, chunk), :]
        place[...] = summed.astype(BF16)
        return [same(place, (d, 2 * j + x)) for j in z_peer]

    def spread_x(g):
        for op in spread[g]:
            op.wait_recv()
        return same(total.at[2 * g : 2 * g + 2, at(half * x, half), :], across_x)

    core, over_y, over_x, over_z, spread = [], [], [], [], []
    for i in range(2):
        product = dot(hidden, cot[:, ci * i : ci * (i + 1)], TN)
        for owner in range(4):
            partial[0, rows * owner + half * i : rows * owner + half * (i + 1), :] = product[
                half * owner : half * (owner + 1)
            ]
    core.append(core_step(0))

    wp = weights[0].reshape(4, 2, half, ci)
    upstream = sum(
        dot(cot[:, ci * i : ci * (i + 1)], wp[:, i].reshape(4 * half, ci), NT) for i in range(2)
    )
    delta[span : span + bins, :] = (upstream * slope).astype(BF16)
    d_after = copy(delta.at[bins : bins + span, :], delta.at[:span, :], after)
    d_before = copy(delta.at[span : 2 * span, :], delta.at[span + bins :, :], before)
    mine = delta[span : span + bins, :]
    for k in range(3):
        partial[1 + k] = dot(act[span * k : span * k + bins, :], mine, TN)
        core.append(core_step(1 + k))
        over_y.append(y_step(k))
    over_y.append(y_step(3))
    over_x.append(x_step(0))
    over_x.append(x_step(1))

    d_after.wait_recv()
    d_before.wait_recv()
    top = jnp.where(s == 0, 0.0, delta[:span, :].astype(F32)).astype(BF16)
    bottom = jnp.where(s == seq - 1, 0.0, delta[span + bins :, :].astype(F32)).astype(BF16)
    padded = jnp.concatenate([top, mine, bottom], axis=0)
    grad = sum(dot(padded[span * (2 - k) : span * (2 - k) + bins], weights[1 + k], NT) for k in range(3))
    normal, scale = normed(x_ref[...].astype(F32))
    grad = grad * gelu_and_slope(normal)[1]
    inner = scale * (grad - normal * jnp.mean(normal * grad, axis=-1, keepdims=True))
    gin_ref[...] = (cot_ref[...].astype(F32) + inner).astype(BF16)

    over_x.append(x_step(2))
    over_z.append(z_step(0))
    over_x.append(x_step(3))
    spread.append(spread_z(0))
    over_z.append(z_step(1))
    last = [spread_x(0)]
    spread.append(spread_z(1))
    last.append(spread_x(1))
    for op in last:
        op.wait_recv()
    grads_ref[...] = total[...]
    for op in sent:
        op.wait_send()


def fused(mesh, inputs, cotangent, dilated_kernel_weight, point_weight):
    seq = mesh.shape["seq"]
    nz = seq // 2
    _, bins, channels = inputs.shape
    rows, taps, ci = dilated_kernel_weight.shape
    half, chunk, pieces, owners = rows // 2, rows // nz, taps + 1, mesh.shape["dp"]
    copies = 5 * (pieces // 2) + 4 + 3 * pieces + (pieces // 2) * (2 * (nz - 1) + 1)
    grad_input, grads = pl.pallas_call(
        functools.partial(fused_kernel, seq),
        out_shape=(
            jax.ShapeDtypeStruct((bins, channels), BF16),
            jax.ShapeDtypeStruct((pieces, rows, ci), BF16),
        ),
        in_specs=[pl.BlockSpec(memory_space=pltpu.VMEM)] * 4,
        out_specs=(pl.BlockSpec(memory_space=pltpu.VMEM),) * 2,
        scratch_shapes=[
            pltpu.VMEM((pieces, owners * rows, ci), BF16),
            pltpu.VMEM((2, DILATION_SPAN, channels), BF16),
            pltpu.VMEM((bins + 2 * DILATION_SPAN, channels), BF16),
            pltpu.VMEM((bins + 2 * DILATION_SPAN, ci), BF16),
            pltpu.VMEM((pieces, owners * rows, ci), F32),
            pltpu.VMEM((pieces, 2 * rows, ci), BF16),
            pltpu.VMEM((pieces, 2 * rows, ci), BF16),
            pltpu.VMEM((pieces, rows, ci), BF16),
            pltpu.VMEM((pieces, rows, ci), BF16),
            pltpu.VMEM((pieces, rows, ci), F32),
            pltpu.VMEM((pieces, half, ci), BF16),
            pltpu.VMEM((pieces, half, ci), BF16),
            pltpu.VMEM((pieces, half, ci), F32),
            pltpu.VMEM((pieces, half, ci), BF16),
            pltpu.VMEM((pieces // 2, nz - 1, chunk, ci), BF16),
            pltpu.VMEM((pieces, rows, ci), BF16),
            pltpu.SemaphoreType.DMA((copies,)),
            pltpu.SemaphoreType.DMA((copies,)),
        ],
        compiler_params=pltpu.CompilerParams(
            collective_id=0, has_side_effects=True, vmem_limit_bytes=48 * 1024 * 1024
        ),
    )(inputs[0], cotangent[0], jnp.transpose(dilated_kernel_weight, (1, 0, 2)), point_weight)
    conv = jnp.transpose(grads[1:], (1, 0, 2)).astype(F32)
    point = jnp.concatenate([grads[0, :half], grads[0, half:]], axis=1).astype(F32)
    return grad_input[None], conv, point


def solution(mesh):
    dp, seq = mesh.shape["dp"], mesh.shape["seq"]

    def step(inputs, cotangent, dilated_kernel_weight, point_weight):
        rows, taps, ci = dilated_kernel_weight.shape
        nz = seq // 2
        pairs = dp == 4 and seq % 4 == 0 and inputs.shape[0] == 1 and taps == 3
        even = rows % 32 == 0 and rows % (16 * nz) == 0
        shapes = 2 * point_weight.shape[0] == rows and point_weight.shape[1] == 2 * ci
        if pairs and even and shapes:
            return fused(mesh, inputs, cotangent, dilated_kernel_weight, point_weight)
        return per_device(inputs, cotangent, dilated_kernel_weight, point_weight)

    return jax.shard_map(
        step,
        mesh=mesh,
        in_specs=(P("dp", "seq", None), P("dp", "seq", None), P("dp", None, None), P("dp", None)),
        out_specs=(P("dp", "seq", None), P("dp", None, None), P("dp", None)),
        check_vma=False,
    )
```

```python
import functools

import jax
import jax.numpy as jnp
from jax import lax
from jax.experimental import pallas as pl
from jax.experimental.pallas import tpu as pltpu
from jax.sharding import PartitionSpec as P

DILATION_SPAN = 32
MESH = pl.DeviceIdType.MESH
F32, BF16 = jnp.float32, jnp.bfloat16
GELU_SCALE, GELU_CUBIC = (2.0 / jnp.pi) ** 0.5, 0.044715


def extended(x, sides, width):
    for axis, dim in sides:
        size, length = (lax.axis_size(axis), x.shape[dim])
        up = [(i, (i + 1) % size) for i in range(size - 1)]
        down = [(j, i) for i, j in up]
        last = lax.slice_in_dim(x, length - width, length, axis=dim)
        initial = lax.slice_in_dim(x, 0, width, axis=dim)
        before = lax.ppermute(last, axis, up)
        after = lax.ppermute(initial, axis, down)
        x = jnp.concatenate([before, x, after], axis=dim)
    return x


def gelu_apply(values):
    return jax.nn.gelu(values, approximate=True)


def rms_normed(values):
    return values * lax.rsqrt(jnp.mean(values * values, axis=-1, keepdims=True) + 1e-06)


def conv_forward(padded_activation, weight_full, output_length):
    return sum(
        (
            jnp.einsum(
                "amv,vb->amb",
                padded_activation[
                    :,
                    kernel_tap_index * DILATION_SPAN : kernel_tap_index * DILATION_SPAN
                    + output_length,
                ],
                weight_full[:, kernel_tap_index, :],
                preferred_element_type=jnp.float32,
            )
            for kernel_tap_index in range(3)
        )
    )


def conv_weight_grad(padded_activation, delta_rows, input_length):
    return jnp.stack(
        [
            jnp.einsum(
                "hyr,hyk->rk",
                padded_activation[
                    :,
                    kernel_tap_index * DILATION_SPAN : kernel_tap_index * DILATION_SPAN
                    + input_length,
                ],
                delta_rows,
                preferred_element_type=jnp.float32,
            )
            for kernel_tap_index in range(3)
        ],
        axis=1,
    )


def conv_backward(padded_delta, weight_full, input_length):
    return sum(
        (
            jnp.einsum(
                "mfi,xi->mfx",
                padded_delta[
                    :,
                    (2 - kernel_tap_index) * DILATION_SPAN : (2 - kernel_tap_index) * DILATION_SPAN
                    + input_length,
                ],
                weight_full[:, kernel_tap_index, :],
                preferred_element_type=jnp.float32,
            )
            for kernel_tap_index in range(3)
        )
    )


def per_device(inputs, cotangent, dilated_kernel_weight, point_weight):
    conv_full, pointwise_full_weight = (
        lax.all_gather(dilated_kernel_weight, "dp", axis=0, tiled=True),
        lax.all_gather(point_weight, "dp", axis=0, tiled=True),
    )
    input_length = inputs.shape[1]
    normal, pull_norm = jax.vjp(rms_normed, inputs.astype(jnp.float32))
    activated_hidden, pull_act = jax.vjp(gelu_apply, normal)
    padded_activation = extended(
        activated_hidden.astype(jnp.bfloat16), (("seq", 1),), DILATION_SPAN
    )
    preactivation = conv_forward(padded_activation, conv_full, input_length)
    hidden, pull_hidden = jax.vjp(gelu_apply, preactivation)
    hidden_halfprec = hidden.astype(jnp.bfloat16)
    pointwise_weight_gradient = jnp.einsum(
        "xth,xtr->hr", hidden_halfprec, cotangent, preferred_element_type=jnp.float32
    )
    upstream_gradient = jnp.einsum(
        "pqy,oy->pqo", cotangent, pointwise_full_weight, preferred_element_type=jnp.float32
    )
    delta_rows = pull_hidden(upstream_gradient)[0].astype(jnp.bfloat16)
    kernel_weight_gradient = conv_weight_grad(padded_activation, delta_rows, input_length)
    padded_delta = extended(delta_rows, (("seq", 1),), DILATION_SPAN)
    activation_gradient = conv_backward(padded_delta, conv_full, input_length)
    grad_normal = pull_act(activation_gradient)[0]
    grad_inner = pull_norm(grad_normal)[0]
    grad_input = (cotangent.astype(jnp.float32) + grad_inner).astype(jnp.bfloat16)
    owned_conv, owned_point = (
        lax.psum_scatter(kernel_weight_gradient, "dp", scatter_dimension=0, tiled=True),
        lax.psum_scatter(pointwise_weight_gradient, "dp", scatter_dimension=0, tiled=True),
    )
    owned_conv, owned_point = lax.psum((owned_conv, owned_point), "seq")
    return (grad_input, owned_conv, owned_point)


def gelu_and_slope(v):
    square = v * v
    t = jnp.tanh(GELU_SCALE * v * (1.0 + GELU_CUBIC * square))
    half = 0.5 * (1.0 + t)
    slope = half + 0.5 * GELU_SCALE * v * (1.0 - t * t) * (1.0 + 3.0 * GELU_CUBIC * square)
    return v * half, slope


def normed(values):
    scale = lax.rsqrt(jnp.mean(values * values, axis=-1, keepdims=True) + 1e-06)
    return values * scale, scale


def dot(a, b, contract):
    return lax.dot_general(a, b, (contract, ((), ())), preferred_element_type=F32)


NN, NT, TN = ((1,), (0,)), ((1,), (1,)), ((0,), (0,))


def fused_kernel(
    seq,
    x_hbm,
    cot_hbm,
    wk_ref,
    wp_ref,
    gin_ref,
    grads_ref,
    weights,
    x_ref,
    cot_ref,
    x_halo,
    act,
    normal_ref,
    slope_ref,
    delta,
    partial,
    core_out,
    core_in,
    first_out,
    first_in,
    first_own,
    second_out,
    second_in,
    z_own,
    z_out,
    z_in,
    total,
    local_sem,
    send_sem,
    recv_sem,
):
    span = DILATION_SPAN
    bins, channels = x_hbm.shape
    pieces, _, ci = weights.shape
    rows = wk_ref.shape[1]
    half = rows // 2
    nz = seq // 2
    chunk = rows // nz
    d, s = lax.axis_index("dp"), lax.axis_index("seq")
    y, c = d // 2, d % 2
    z, x = s // 2, s % 2
    sibling = (2 * y + 1 - c, s)
    across_y = (2 * (1 - y) + c, s)
    across_x = (d, 2 * z + 1 - x)
    after, before = (d, (s + 1) % seq), (d, (s + seq - 1) % seq)
    z_peer = [(z + r) % nz for r in range(1, nz)]

    count = [0]
    sent = []

    def copy(src, dst, device):
        i = count[0]
        count[0] += 1
        op = pltpu.make_async_remote_copy(
            src_ref=src,
            dst_ref=dst,
            send_sem=send_sem.at[i],
            recv_sem=recv_sem.at[i],
            device_id=device,
            device_id_type=MESH,
        )
        op.start()
        sent.append(op)
        return op

    def at(start, size, step=16):
        return pl.ds(pl.multiple_of(start, step), size)

    barrier = pltpu.get_barrier_semaphore()
    peers = [sibling, across_y, across_x, after, before] + [(d, 2 * j + x) for j in z_peer]
    for device in peers:
        pl.semaphore_signal(barrier, inc=1, device_id=device, device_id_type=MESH)

    own = rows * d
    wp_half = [wp_ref.at[:, :ci], wp_ref.at[:, ci:]]
    local = [
        (x_hbm, x_ref),
        (cot_hbm, cot_ref),
        (wp_half[0], weights.at[0, at(own, half), :]),
        (wp_half[1], weights.at[0, at(own + half, half), :]),
        (wk_ref, weights.at[1:, at(own, rows), :]),
    ]
    local = [pltpu.make_async_copy(a, b, local_sem.at[i]) for i, (a, b) in enumerate(local)]
    for op in local:
        op.start()
    pl.semaphore_wait(barrier, len(peers))

    def same(ref, device):
        return copy(ref, ref, device)

    def block(p, start, size):
        return weights.at[p, at(start, size), :]

    mine = block(0, own + half * x, half)
    w_y = [copy(wp_ref.at[:, at(ci * x, ci, 128)], mine, across_y)]
    halo_after = copy(x_hbm.at[bins - span :, :], x_halo.at[0], after)
    halo_before = copy(x_hbm.at[:span, :], x_halo.at[1], before)
    for k in range(3):
        mine = block(1 + k, own + half * x, half)
        w_y.append(copy(wk_ref.at[k, at(half * x, half), :], mine, across_y))
    w_core = [copy(wp_half[i], block(0, own + half * i, half), sibling) for i in range(2)]
    w_core.append(copy(wk_ref, weights.at[1:, at(own, rows), :], sibling))

    local[0].wait()
    normal, _ = normed(x_ref[...].astype(F32))
    value, slope = gelu_and_slope(normal)
    act[span : span + bins, :] = value.astype(BF16)
    normal_ref[...] = normal
    slope_ref[...] = slope

    other = rows * (2 * (1 - y) + c)
    w_x, w_pass, w_last = [], [], []

    def pass_y(p):
        w_y[p].wait_recv()
        w_x.append(same(block(p, other + half * x, half), across_x))
        w_pass.append(same(block(p, other + half * x, half), sibling))

    def pass_x(p):
        w_x[p].wait_recv()
        w_last.append(same(block(p, other + half * (1 - x), half), sibling))

    def ready(p):
        w_pass[p].wait_recv()
        w_last[p].wait_recv()

    pass_y(0)
    pass_y(1)
    halo_after.wait_recv()
    halo_before.wait_recv()
    for i, edge, start in ((0, 0, 0), (1, seq - 1, span + bins)):
        side, _ = normed(x_halo[i].astype(F32))
        side = gelu_and_slope(side)[0]
        act[start : start + span, :] = jnp.where(s == edge, 0.0, side).astype(BF16)
    pass_x(0)
    pass_y(2)
    pass_x(1)
    for op in local[1:]:
        op.wait()
    for op in w_core:
        op.wait_recv()
    pass_y(3)
    ready(0)
    cot = cot_ref[...]
    wp = weights[0].reshape(4, 2, half, ci)
    upstream = sum(
        dot(cot[:, ci * i : ci * (i + 1)], wp[:, i].reshape(4 * half, ci), NT) for i in range(2)
    )
    pass_x(2)
    ready(1)
    preact = dot(act[:bins, :], weights[1], NN)
    pass_x(3)
    ready(2)
    preact += dot(act[span : span + bins, :], weights[2], NN)
    ready(3)
    preact += dot(act[2 * span : 2 * span + bins, :], weights[3], NN)
    hidden, slope = gelu_and_slope(preact)
    hidden = hidden.astype(BF16)

    def core_step(p):
        for i in range(2):
            core_out[p, rows * i : rows * (i + 1), :] = partial[
                p, at(rows * (2 * i + 1 - c), rows), :
            ].astype(BF16)
        return copy(core_out.at[p], core_in.at[p], sibling)

    def first_step(p):
        core[p].wait_recv()
        if p % 2 == 0:
            away, stay = [(2 * (1 - y) + c, 1 - y, 0, rows)], [(d, y, 0, rows)]
        else:
            away = [(2 * i + c, i, half * (1 - x), half) for i in range(2)]
            stay = [(2 * i + c, i, half * x, half) for i in range(2)]

        def summed(owner, slot, row, size):
            theirs = core_in[p, at(rows * slot + row, size), :].astype(F32)
            return partial[p, at(rows * owner + row, size), :] + theirs

        for i, part in enumerate(away):
            first_out[p, part[3] * i : part[3] * (i + 1), :] = summed(*part).astype(BF16)
        op = copy(first_out.at[p], first_in.at[p], across_x if p % 2 else across_y)
        for i, part in enumerate(stay):
            first_own[p, part[3] * i : part[3] * (i + 1), :] = summed(*part)
        return op

    def second_step(p):
        first[p].wait_recv()
        side, device = (y, across_y) if p % 2 else (x, across_x)
        theirs, ours = at(half * (1 - side), half), at(half * side, half)
        second_out[p] = (first_own[p, theirs, :] + first_in[p, theirs, :].astype(F32)).astype(BF16)
        op = copy(second_out.at[p], second_in.at[p], device)
        z_own[p] = first_own[p, ours, :] + first_in[p, ours, :].astype(F32)
        return op

    def z_step(g):
        for p in (2 * g, 2 * g + 1):
            second[p].wait_recv()
            z_own[p] = z_own[p] + second_in[p].astype(F32)
            z_out[p] = z_own[p].astype(BF16)
        ops = []
        for r, j in enumerate(z_peer):
            piece, row = j // (nz // 2), chunk * (j % (nz // 2))
            ops.append(copy(z_out.at[2 * g + piece, at(row, chunk), :], z_in.at[g, r], (d, 2 * j + x)))
        return ops

    def spread_z(g):
        piece, row = 2 * g + z // (nz // 2), chunk * (z % (nz // 2))
        summed = z_own[piece, at(row, chunk), :]
        for r in range(nz - 1):
            over_z[g][r].wait_recv()
            summed = summed + z_in[g, r].astype(F32)
        place = total.at[piece, at(half * x + row, chunk), :]
        place[...] = summed.astype(BF16)
        ops = [same(place, (d, 2 * j + x)) for j in z_peer]
        last.append(same(place, across_x))
        return ops

    def spread_x(g):
        for r in range(1, nz):
            spread[g][r - 1].wait_recv()
            j = (z + nz - r) % nz
            piece, row = 2 * g + j // (nz // 2), chunk * (j % (nz // 2))
            last.append(same(total.at[piece, at(half * x + row, chunk), :], across_x))

    core, first, second, over_z, spread, last = [], [], [], [], [], []
    for i in range(2):
        product = dot(hidden, cot[:, ci * i : ci * (i + 1)], TN)
        for owner in range(4):
            partial[0, rows * owner + half * i : rows * owner + half * (i + 1), :] = product[
                half * owner : half * (owner + 1)
            ]
    core.append(core_step(0))

    delta[span : span + bins, :] = (upstream * slope).astype(BF16)
    d_after = copy(delta.at[bins : bins + span, :], delta.at[:span, :], after)
    d_before = copy(delta.at[span : 2 * span, :], delta.at[span + bins :, :], before)
    mine = delta[span : span + bins, :]
    for k in range(3):
        partial[1 + k] = dot(act[span * k : span * k + bins, :], mine, TN)
        core.append(core_step(1 + k))
        first.append(first_step(k))
    first.append(first_step(3))

    d_after.wait_recv()
    d_before.wait_recv()
    top = jnp.where(s == 0, 0.0, delta[:span, :].astype(F32)).astype(BF16)
    bottom = jnp.where(s == seq - 1, 0.0, delta[span + bins :, :].astype(F32)).astype(BF16)
    padded = jnp.concatenate([top, mine, bottom], axis=0)
    grad = sum(dot(padded[span * (2 - k) : span * (2 - k) + bins], weights[1 + k], NT) for k in range(3))
    second.append(second_step(0))
    second.append(second_step(1))
    normal = normal_ref[...]
    _, scale = normed(x_ref[...].astype(F32))
    grad = grad * slope_ref[...]
    inner = scale * (grad - normal * jnp.mean(normal * grad, axis=-1, keepdims=True))
    gin_ref[...] = (cot_ref[...].astype(F32) + inner).astype(BF16)

    over_z.append(z_step(0))
    second.append(second_step(2))
    second.append(second_step(3))
    spread.append(spread_z(0))
    over_z.append(z_step(1))
    spread_x(0)
    spread.append(spread_z(1))
    spread_x(1)
    for op in last:
        op.wait_recv()
    grads_ref[...] = total[...]
    for op in sent:
        op.wait_send()


def fused(mesh, inputs, cotangent, dilated_kernel_weight, point_weight):
    seq = mesh.shape["seq"]
    nz = seq // 2
    _, bins, channels = inputs.shape
    rows, taps, ci = dilated_kernel_weight.shape
    half, chunk, pieces, owners = rows // 2, rows // nz, taps + 1, mesh.shape["dp"]
    copies = 4 * pieces + 3 + 4 + 3 * pieces + (pieces // 2) * (3 * nz - 2)
    grad_input, grads = pl.pallas_call(
        functools.partial(fused_kernel, seq),
        out_shape=(
            jax.ShapeDtypeStruct((bins, channels), BF16),
            jax.ShapeDtypeStruct((pieces, rows, ci), BF16),
        ),
        in_specs=[pl.BlockSpec(memory_space=pltpu.HBM)] * 4,
        out_specs=(pl.BlockSpec(memory_space=pltpu.VMEM),) * 2,
        scratch_shapes=[
            pltpu.VMEM((pieces, owners * rows, ci), BF16),
            pltpu.VMEM((bins, channels), BF16),
            pltpu.VMEM((bins, channels), BF16),
            pltpu.VMEM((2, DILATION_SPAN, channels), BF16),
            pltpu.VMEM((bins + 2 * DILATION_SPAN, channels), BF16),
            pltpu.VMEM((bins, channels), F32),
            pltpu.VMEM((bins, channels), F32),
            pltpu.VMEM((bins + 2 * DILATION_SPAN, ci), BF16),
            pltpu.VMEM((pieces, owners * rows, ci), F32),
            pltpu.VMEM((pieces, 2 * rows, ci), BF16),
            pltpu.VMEM((pieces, 2 * rows, ci), BF16),
            pltpu.VMEM((pieces, rows, ci), BF16),
            pltpu.VMEM((pieces, rows, ci), BF16),
            pltpu.VMEM((pieces, rows, ci), F32),
            pltpu.VMEM((pieces, half, ci), BF16),
            pltpu.VMEM((pieces, half, ci), BF16),
            pltpu.VMEM((pieces, half, ci), F32),
            pltpu.VMEM((pieces, half, ci), BF16),
            pltpu.VMEM((pieces // 2, nz - 1, chunk, ci), BF16),
            pltpu.VMEM((pieces, rows, ci), BF16),
            pltpu.SemaphoreType.DMA((5,)),
            pltpu.SemaphoreType.DMA((copies,)),
            pltpu.SemaphoreType.DMA((copies,)),
        ],
        compiler_params=pltpu.CompilerParams(
            collective_id=0, has_side_effects=True, vmem_limit_bytes=48 * 1024 * 1024
        ),
    )(inputs[0], cotangent[0], jnp.transpose(dilated_kernel_weight, (1, 0, 2)), point_weight)
    conv = jnp.transpose(grads[1:], (1, 0, 2)).astype(F32)
    point = jnp.concatenate([grads[0, :half], grads[0, half:]], axis=1).astype(F32)
    return grad_input[None], conv, point


def solution(mesh):
    dp, seq = mesh.shape["dp"], mesh.shape["seq"]

    def step(inputs, cotangent, dilated_kernel_weight, point_weight):
        rows, taps, ci = dilated_kernel_weight.shape
        nz = seq // 2
        pairs = dp == 4 and seq % 4 == 0 and inputs.shape[0] == 1 and taps == 3
        even = rows % 32 == 0 and rows % (16 * nz) == 0
        shapes = 2 * point_weight.shape[0] == rows and point_weight.shape[1] == 2 * ci
        if pairs and even and shapes:
            return fused(mesh, inputs, cotangent, dilated_kernel_weight, point_weight)
        return per_device(inputs, cotangent, dilated_kernel_weight, point_weight)

    return jax.shard_map(
        step,
        mesh=mesh,
        in_specs=(P("dp", "seq", None), P("dp", "seq", None), P("dp", None, None), P("dp", None)),
        out_specs=(P("dp", "seq", None), P("dp", None, None), P("dp", None)),
        check_vma=False,
    )
```

```python
import functools

import jax
import jax.numpy as jnp
from jax import lax
from jax.experimental import pallas as pl
from jax.experimental.pallas import tpu as pltpu
from jax.sharding import PartitionSpec as P

DILATION_SPAN = 32
MESH = pl.DeviceIdType.MESH
F32, BF16 = jnp.float32, jnp.bfloat16
GELU_SCALE, GELU_CUBIC = (2.0 / jnp.pi) ** 0.5, 0.044715


def extended(x, sides, width):
    for axis, dim in sides:
        size, length = (lax.axis_size(axis), x.shape[dim])
        up = [(i, (i + 1) % size) for i in range(size - 1)]
        down = [(j, i) for i, j in up]
        last = lax.slice_in_dim(x, length - width, length, axis=dim)
        initial = lax.slice_in_dim(x, 0, width, axis=dim)
        before = lax.ppermute(last, axis, up)
        after = lax.ppermute(initial, axis, down)
        x = jnp.concatenate([before, x, after], axis=dim)
    return x


def gelu_apply(values):
    return jax.nn.gelu(values, approximate=True)


def rms_normed(values):
    return values * lax.rsqrt(jnp.mean(values * values, axis=-1, keepdims=True) + 1e-06)


def conv_forward(padded_activation, weight_full, output_length):
    return sum(
        (
            jnp.einsum(
                "amv,vb->amb",
                padded_activation[
                    :,
                    kernel_tap_index * DILATION_SPAN : kernel_tap_index * DILATION_SPAN
                    + output_length,
                ],
                weight_full[:, kernel_tap_index, :],
                preferred_element_type=jnp.float32,
            )
            for kernel_tap_index in range(3)
        )
    )


def conv_weight_grad(padded_activation, delta_rows, input_length):
    return jnp.stack(
        [
            jnp.einsum(
                "hyr,hyk->rk",
                padded_activation[
                    :,
                    kernel_tap_index * DILATION_SPAN : kernel_tap_index * DILATION_SPAN
                    + input_length,
                ],
                delta_rows,
                preferred_element_type=jnp.float32,
            )
            for kernel_tap_index in range(3)
        ],
        axis=1,
    )


def conv_backward(padded_delta, weight_full, input_length):
    return sum(
        (
            jnp.einsum(
                "mfi,xi->mfx",
                padded_delta[
                    :,
                    (2 - kernel_tap_index) * DILATION_SPAN : (2 - kernel_tap_index) * DILATION_SPAN
                    + input_length,
                ],
                weight_full[:, kernel_tap_index, :],
                preferred_element_type=jnp.float32,
            )
            for kernel_tap_index in range(3)
        )
    )


def per_device(inputs, cotangent, dilated_kernel_weight, point_weight):
    conv_full, pointwise_full_weight = (
        lax.all_gather(dilated_kernel_weight, "dp", axis=0, tiled=True),
        lax.all_gather(point_weight, "dp", axis=0, tiled=True),
    )
    input_length = inputs.shape[1]
    normal, pull_norm = jax.vjp(rms_normed, inputs.astype(jnp.float32))
    activated_hidden, pull_act = jax.vjp(gelu_apply, normal)
    padded_activation = extended(
        activated_hidden.astype(jnp.bfloat16), (("seq", 1),), DILATION_SPAN
    )
    preactivation = conv_forward(padded_activation, conv_full, input_length)
    hidden, pull_hidden = jax.vjp(gelu_apply, preactivation)
    hidden_halfprec = hidden.astype(jnp.bfloat16)
    pointwise_weight_gradient = jnp.einsum(
        "xth,xtr->hr", hidden_halfprec, cotangent, preferred_element_type=jnp.float32
    )
    upstream_gradient = jnp.einsum(
        "pqy,oy->pqo", cotangent, pointwise_full_weight, preferred_element_type=jnp.float32
    )
    delta_rows = pull_hidden(upstream_gradient)[0].astype(jnp.bfloat16)
    kernel_weight_gradient = conv_weight_grad(padded_activation, delta_rows, input_length)
    padded_delta = extended(delta_rows, (("seq", 1),), DILATION_SPAN)
    activation_gradient = conv_backward(padded_delta, conv_full, input_length)
    grad_normal = pull_act(activation_gradient)[0]
    grad_inner = pull_norm(grad_normal)[0]
    grad_input = (cotangent.astype(jnp.float32) + grad_inner).astype(jnp.bfloat16)
    owned_conv, owned_point = (
        lax.psum_scatter(kernel_weight_gradient, "dp", scatter_dimension=0, tiled=True),
        lax.psum_scatter(pointwise_weight_gradient, "dp", scatter_dimension=0, tiled=True),
    )
    owned_conv, owned_point = lax.psum((owned_conv, owned_point), "seq")
    return (grad_input, owned_conv, owned_point)


def gelu_and_slope(v):
    square = v * v
    t = jnp.tanh(GELU_SCALE * v * (1.0 + GELU_CUBIC * square))
    half = 0.5 * (1.0 + t)
    slope = half + 0.5 * GELU_SCALE * v * (1.0 - t * t) * (1.0 + 3.0 * GELU_CUBIC * square)
    return v * half, slope


def normed(values):
    scale = lax.rsqrt(jnp.mean(values * values, axis=-1, keepdims=True) + 1e-06)
    return values * scale, scale


def dot(a, b, contract):
    return lax.dot_general(a, b, (contract, ((), ())), preferred_element_type=F32)


NN, NT, TN = ((1,), (0,)), ((1,), (1,)), ((0,), (0,))


def fused_kernel(
    seq,
    x_hbm,
    cot_hbm,
    wk_ref,
    wp_ref,
    gin_ref,
    grads_ref,
    weights,
    x_ref,
    cot_ref,
    x_halo,
    act,
    normal_ref,
    slope_ref,
    delta,
    partial,
    core_out,
    core_in,
    first_out,
    first_in,
    first_own,
    second_out,
    second_in,
    z_own,
    z_out,
    z_in,
    total,
    local_sem,
    send_sem,
    recv_sem,
):
    span = DILATION_SPAN
    bins, channels = x_hbm.shape
    pieces, _, ci = weights.shape
    rows = wk_ref.shape[1]
    half = rows // 2
    nz = seq // 2
    chunk = rows // nz
    d, s = lax.axis_index("dp"), lax.axis_index("seq")
    y, c = d // 2, d % 2
    z, x = s // 2, s % 2
    sibling = (2 * y + 1 - c, s)
    across_y = (2 * (1 - y) + c, s)
    across_x = (d, 2 * z + 1 - x)
    after, before = (d, (s + 1) % seq), (d, (s + seq - 1) % seq)
    z_peer = [(z + r) % nz for r in range(1, nz)]

    count = [0]
    sent = []

    def copy(src, dst, device):
        i = count[0]
        count[0] += 1
        op = pltpu.make_async_remote_copy(
            src_ref=src,
            dst_ref=dst,
            send_sem=send_sem.at[i],
            recv_sem=recv_sem.at[i],
            device_id=device,
            device_id_type=MESH,
        )
        op.start()
        sent.append(op)
        return op

    def at(start, size, step=16):
        return pl.ds(pl.multiple_of(start, step), size)

    barrier = pltpu.get_barrier_semaphore()
    peers = [sibling, across_y, across_x, after, before] + [(d, 2 * j + x) for j in z_peer]
    for device in peers:
        pl.semaphore_signal(barrier, inc=1, device_id=device, device_id_type=MESH)

    own = rows * d
    wp_half = [wp_ref.at[:, :ci], wp_ref.at[:, ci:]]
    local = [
        (x_hbm, x_ref),
        (cot_hbm, cot_ref),
        (wp_half[0], weights.at[0, at(own, half), :]),
        (wp_half[1], weights.at[0, at(own + half, half), :]),
        (wk_ref, weights.at[1:, at(own, rows), :]),
    ]
    local = [pltpu.make_async_copy(a, b, local_sem.at[i]) for i, (a, b) in enumerate(local)]
    for op in local:
        op.start()
    pl.semaphore_wait(barrier, len(peers))

    def same(ref, device):
        return copy(ref, ref, device)

    def block(p, start, size):
        return weights.at[p, at(start, size), :]

    mine = block(0, own + half * x, half)
    w_y = [copy(wp_ref.at[:, at(ci * x, ci, 128)], mine, across_y)]
    halo_after = copy(x_hbm.at[bins - span :, :], x_halo.at[0], after)
    halo_before = copy(x_hbm.at[:span, :], x_halo.at[1], before)
    for k in range(3):
        mine = block(1 + k, own + half * x, half)
        w_y.append(copy(wk_ref.at[k, at(half * x, half), :], mine, across_y))
    w_core = [copy(wp_half[i], block(0, own + half * i, half), sibling) for i in range(2)]
    w_core.append(copy(wk_ref, weights.at[1:, at(own, rows), :], sibling))

    local[0].wait()
    normal, _ = normed(x_ref[...].astype(F32))
    value, slope = gelu_and_slope(normal)
    act[span : span + bins, :] = value.astype(BF16)
    normal_ref[...] = normal
    slope_ref[...] = slope

    other = rows * (2 * (1 - y) + c)
    w_x, w_pass, w_last = [], [], []

    def pass_y(p):
        w_y[p].wait_recv()
        w_x.append(same(block(p, other + half * x, half), across_x))
        w_pass.append(same(block(p, other + half * x, half), sibling))

    def pass_x(p):
        w_x[p].wait_recv()
        w_last.append(same(block(p, other + half * (1 - x), half), sibling))

    def ready(p):
        w_pass[p].wait_recv()
        w_last[p].wait_recv()

    pass_y(0)
    pass_y(1)
    halo_after.wait_recv()
    halo_before.wait_recv()
    for i, edge, start in ((0, 0, 0), (1, seq - 1, span + bins)):
        side, _ = normed(x_halo[i].astype(F32))
        side = gelu_and_slope(side)[0]
        act[start : start + span, :] = jnp.where(s == edge, 0.0, side).astype(BF16)
    pass_x(0)
    pass_y(2)
    pass_x(1)
    for op in local[1:]:
        op.wait()
    for op in w_core:
        op.wait_recv()
    pass_y(3)
    ready(0)
    cot = cot_ref[...]
    wp = weights[0].reshape(4, 2, half, ci)
    upstream = sum(
        dot(cot[:, ci * i : ci * (i + 1)], wp[:, i].reshape(4 * half, ci), NT) for i in range(2)
    )
    pass_x(2)
    ready(1)
    preact = dot(act[:bins, :], weights[1], NN)
    pass_x(3)
    ready(2)
    preact += dot(act[span : span + bins, :], weights[2], NN)
    ready(3)
    preact += dot(act[2 * span : 2 * span + bins, :], weights[3], NN)
    hidden, slope = gelu_and_slope(preact)
    hidden = hidden.astype(BF16)

    def core_step(p):
        for i in range(2):
            core_out[p, rows * i : rows * (i + 1), :] = partial[
                p, at(rows * (2 * i + 1 - c), rows), :
            ].astype(BF16)
        return copy(core_out.at[p], core_in.at[p], sibling)

    def first_step(p):
        core[p].wait_recv()
        if p % 2 == 0:
            away, stay = [(2 * (1 - y) + c, 1 - y, 0, rows)], [(d, y, 0, rows)]
        else:
            away = [(2 * i + c, i, half * (1 - x), half) for i in range(2)]
            stay = [(2 * i + c, i, half * x, half) for i in range(2)]

        def summed(owner, slot, row, size):
            theirs = core_in[p, at(rows * slot + row, size), :].astype(F32)
            return partial[p, at(rows * owner + row, size), :] + theirs

        for i, part in enumerate(away):
            first_out[p, part[3] * i : part[3] * (i + 1), :] = summed(*part).astype(BF16)
        op = copy(first_out.at[p], first_in.at[p], across_x if p % 2 else across_y)
        for i, part in enumerate(stay):
            first_own[p, part[3] * i : part[3] * (i + 1), :] = summed(*part)
        return op

    def second_step(p):
        first[p].wait_recv()
        side, device = (y, across_y) if p % 2 else (x, across_x)
        theirs, ours = at(half * (1 - side), half), at(half * side, half)
        second_out[p] = (first_own[p, theirs, :] + first_in[p, theirs, :].astype(F32)).astype(BF16)
        op = copy(second_out.at[p], second_in.at[p], device)
        z_own[p] = first_own[p, ours, :] + first_in[p, ours, :].astype(F32)
        return op

    def z_step(g):
        for p in (2 * g, 2 * g + 1):
            second[p].wait_recv()
            z_own[p] = z_own[p] + second_in[p].astype(F32)
            z_out[p] = z_own[p].astype(BF16)
        ops = []
        for r, j in enumerate(z_peer):
            piece, row = j // (nz // 2), chunk * (j % (nz // 2))
            ops.append(copy(z_out.at[2 * g + piece, at(row, chunk), :], z_in.at[g, r], (d, 2 * j + x)))
        return ops

    def spread_z(g):
        piece, row = 2 * g + z // (nz // 2), chunk * (z % (nz // 2))
        summed = z_own[piece, at(row, chunk), :]
        for r in range(nz - 1):
            over_z[g][r].wait_recv()
            summed = summed + z_in[g, r].astype(F32)
        place = total.at[piece, at(half * x + row, chunk), :]
        place[...] = summed.astype(BF16)
        ops = [same(place, (d, 2 * j + x)) for j in z_peer]
        last.append(same(place, across_x))
        return ops

    def spread_x(g):
        for r in range(1, nz):
            spread[g][r - 1].wait_recv()
            j = (z + nz - r) % nz
            piece, row = 2 * g + j // (nz // 2), chunk * (j % (nz // 2))
            last.append(same(total.at[piece, at(half * x + row, chunk), :], across_x))

    core, first, second, over_z, spread, last = [], [], [], [], [], []
    for i in range(2):
        product = dot(hidden, cot[:, ci * i : ci * (i + 1)], TN)
        for owner in range(4):
            partial[0, rows * owner + half * i : rows * owner + half * (i + 1), :] = product[
                half * owner : half * (owner + 1)
            ]
    core.append(core_step(0))

    delta[span : span + bins, :] = (upstream * slope).astype(BF16)
    d_after = copy(delta.at[bins : bins + span, :], delta.at[:span, :], after)
    d_before = copy(delta.at[span : 2 * span, :], delta.at[span + bins :, :], before)
    mine = delta[span : span + bins, :]
    for k in range(3):
        partial[1 + k] = dot(act[span * k : span * k + bins, :], mine, TN)
        core.append(core_step(1 + k))
        first.append(first_step(k))
    first.append(first_step(3))

    d_after.wait_recv()
    d_before.wait_recv()
    top = jnp.where(s == 0, 0.0, delta[:span, :].astype(F32)).astype(BF16)
    bottom = jnp.where(s == seq - 1, 0.0, delta[span + bins :, :].astype(F32)).astype(BF16)
    padded = jnp.concatenate([top, mine, bottom], axis=0)
    grad = sum(dot(padded[span * (2 - k) : span * (2 - k) + bins], weights[1 + k], NT) for k in range(3))
    second.append(second_step(0))
    second.append(second_step(1))
    normal = normal_ref[...]
    _, scale = normed(x_ref[...].astype(F32))
    grad = grad * slope_ref[...]
    inner = scale * (grad - normal * jnp.mean(normal * grad, axis=-1, keepdims=True))
    gin_ref[...] = (cot_ref[...].astype(F32) + inner).astype(BF16)

    over_z.append(z_step(0))
    second.append(second_step(2))
    second.append(second_step(3))
    spread.append(spread_z(0))
    over_z.append(z_step(1))
    spread_x(0)
    spread.append(spread_z(1))
    spread_x(1)
    for op in last:
        op.wait_recv()
    grads_ref[...] = total[...]
    for op in sent:
        op.wait_send()


def fused(mesh, inputs, cotangent, dilated_kernel_weight, point_weight):
    seq = mesh.shape["seq"]
    nz = seq // 2
    _, bins, channels = inputs.shape
    rows, taps, ci = dilated_kernel_weight.shape
    half, chunk, pieces, owners = rows // 2, rows // nz, taps + 1, mesh.shape["dp"]
    copies = 4 * pieces + 3 + 4 + 3 * pieces + (pieces // 2) * (3 * nz - 2)
    grad_input, grads = pl.pallas_call(
        functools.partial(fused_kernel, seq),
        out_shape=(
            jax.ShapeDtypeStruct((bins, channels), BF16),
            jax.ShapeDtypeStruct((pieces, rows, ci), BF16),
        ),
        in_specs=[pl.BlockSpec(memory_space=pltpu.HBM)] * 4,
        out_specs=(pl.BlockSpec(memory_space=pltpu.VMEM),) * 2,
        scratch_shapes=[
            pltpu.VMEM((pieces, owners * rows, ci), BF16),
            pltpu.VMEM((bins, channels), BF16),
            pltpu.VMEM((bins, channels), BF16),
            pltpu.VMEM((2, DILATION_SPAN, channels), BF16),
            pltpu.VMEM((bins + 2 * DILATION_SPAN, channels), BF16),
            pltpu.VMEM((bins, channels), F32),
            pltpu.VMEM((bins, channels), F32),
            pltpu.VMEM((bins + 2 * DILATION_SPAN, ci), BF16),
            pltpu.VMEM((pieces, owners * rows, ci), F32),
            pltpu.VMEM((pieces, 2 * rows, ci), BF16),
            pltpu.VMEM((pieces, 2 * rows, ci), BF16),
            pltpu.VMEM((pieces, rows, ci), BF16),
            pltpu.VMEM((pieces, rows, ci), BF16),
            pltpu.VMEM((pieces, rows, ci), F32),
            pltpu.VMEM((pieces, half, ci), BF16),
            pltpu.VMEM((pieces, half, ci), BF16),
            pltpu.VMEM((pieces, half, ci), F32),
            pltpu.VMEM((pieces, half, ci), BF16),
            pltpu.VMEM((pieces // 2, nz - 1, chunk, ci), BF16),
            pltpu.VMEM((pieces, rows, ci), BF16),
            pltpu.SemaphoreType.DMA((5,)),
            pltpu.SemaphoreType.DMA((copies,)),
            pltpu.SemaphoreType.DMA((copies,)),
        ],
        compiler_params=pltpu.CompilerParams(
            collective_id=0, has_side_effects=True, vmem_limit_bytes=63 * 1024 * 1024
        ),
    )(inputs[0], cotangent[0], jnp.transpose(dilated_kernel_weight, (1, 0, 2)), point_weight)
    conv = jnp.transpose(grads[1:], (1, 0, 2)).astype(F32)
    point = jnp.concatenate([grads[0, :half], grads[0, half:]], axis=1).astype(F32)
    return grad_input[None], conv, point


def solution(mesh):
    dp, seq = mesh.shape["dp"], mesh.shape["seq"]

    def step(inputs, cotangent, dilated_kernel_weight, point_weight):
        rows, taps, ci = dilated_kernel_weight.shape
        nz = seq // 2
        pairs = dp == 4 and seq % 4 == 0 and inputs.shape[0] == 1 and taps == 3
        even = rows % 32 == 0 and rows % (16 * nz) == 0
        shapes = 2 * point_weight.shape[0] == rows and point_weight.shape[1] == 2 * ci
        if pairs and even and shapes:
            return fused(mesh, inputs, cotangent, dilated_kernel_weight, point_weight)
        return per_device(inputs, cotangent, dilated_kernel_weight, point_weight)

    return jax.shard_map(
        step,
        mesh=mesh,
        in_specs=(P("dp", "seq", None), P("dp", "seq", None), P("dp", None, None), P("dp", None)),
        out_specs=(P("dp", "seq", None), P("dp", None, None), P("dp", None)),
        check_vma=False,
    )
```
